256 devices in a mesh: dp: 32 (over x, z), tensor: 8 (over y, core).
Axes of the slice: x: 4, y: 4, z: 8, core: 2. Of those that a mesh axis runs over, the one named last changes fastest.
Arguments:
- momentum: float32 [32, 128, 28672], P('dp', None, 'tensor'), may hold values from -120 to 120, as said below
- grad: bfloat16 [32, 128, 28672], P('dp', None, 'tensor'), may hold values from -80 to 80, as said below
Outputs:
- new_momentum: float32 [32, 128, 28672], P('dp', None, 'tensor')
- update: float32 [128, 28672], P(None, 'tensor')
The draws below stay inside these ranges and needn't reach their ends.
Inputs may be any that keep to these rules, and one draw needn't show every extreme that they name: `momentum`: scaled entries. `grad`: scaled entries.
All inputs are finite; a program needn't handle non-finite values.
Results may differ from the reference program's by a relative error of at most 0.0003.
Values sent between devices are 32-bit elements; how exact they have to be, the bound alone decides.
No kernel may reach another device: no remote copies, remote signals or barrier semaphores. Data moves between devices by JAX's collectives and lax.ppermute only.
A program may use at most 64 MiB of HBM per device.

```python
import math
import jax
import jax.numpy as jnp
from jax import lax

FF = 28672
ROWS = 128
REPLICAS = 32


def scale_table(key):
    first, second = jax.random.split(key)
    row_scale = jnp.exp(jax.random.uniform(first, (ROWS,), minval=0.0, maxval=math.log(10.0)))
    col_scale = jnp.exp(jax.random.uniform(second, (FF,), minval=0.0, maxval=math.log(10.0)) + math.log(3.0) * jnp.arange(FF, dtype=jnp.float32) / FF)
    return row_scale[:, None] * col_scale[None, :] / 20.0


def draw_momentum(key, part):
    table = scale_table(key)
    key = jax.random.fold_in(key, 2)
    values = jax.random.truncated_normal(key, -4.0, 4.0, (REPLICAS, ROWS, FF))
    return (2.0 * values * table[None]).astype(jnp.float32)


def draw_grad(key, part):
    table = scale_table(key)
    key = jax.random.fold_in(key, 1)
    values = jax.random.truncated_normal(key, -4.0, 4.0, (REPLICAS, ROWS, FF))
    return (values * table[None]).astype(jnp.bfloat16)


def setup_inputs(seed: int = 0) -> dict:
    splits = jax.random.split(jax.random.key(seed), 3)
    return {
        "momentum": draw_momentum(jax.random.fold_in(splits[2], 71), 0),
        "grad": draw_grad(jax.random.fold_in(splits[2], 71), 0),
    }


def dct_lowband():
    samples = jnp.arange(32, dtype=jnp.float32)
    freqs = jnp.arange(8, dtype=jnp.float32)
    weights = jnp.where(freqs == 0.0, math.sqrt(1.0 / 32.0), math.sqrt(2.0 / 32.0))
    return weights[:, None] * jnp.cos(math.pi * (2.0 * samples[None, :] + 1.0) * freqs[:, None] / 64.0)

def encode(lowband, field):
    tiled = field.reshape(ROWS // 32, 32, FF // 32, 32)
    return jnp.einsum('kn,anbm,lm->abkl', lowband, tiled, lowband, precision=lax.Precision.HIGHEST)

def decode(lowband, coeffs):
    tiled = jnp.einsum('kn,abkl,lm->anbm', lowband, coeffs, lowband, precision=lax.Precision.HIGHEST)
    return tiled.reshape(ROWS, FF)

def reference(momentum, grad):
    lowband = dct_lowband()

    def per_replica(pair):
        moment = 0.999 * pair[0] + pair[1].astype(jnp.float32)
        bands = encode(lowband, moment)
        return (moment - decode(lowband, bands), bands)
    new_momentum, bands = lax.map(per_replica, (momentum, grad))
    summed_bands = lax.optimization_barrier(jnp.sum(bands, axis=0))
    energy = jnp.sum(summed_bands * summed_bands)
    update = decode(lowband, summed_bands) / jnp.sqrt(energy / (ROWS * FF) + 1e-06)
    return (new_momentum, update)
```

```python
import math

import jax
import jax.numpy as jnp
import ml_dtypes
import numpy as np
from jax import lax
from jax.experimental import pallas as pl
from jax.experimental.pallas import tpu as pltpu
from jax.sharding import PartitionSpec as P

FF = 28672
ROWS = 128
CHUNK = 512
F32 = jnp.float32
BF16 = jnp.bfloat16
HBM = pl.BlockSpec(memory_space=pltpu.HBM)
VMEM = pl.BlockSpec(memory_space=pltpu.VMEM)


def lowband():
    samples = np.arange(32, dtype=np.float64)
    freqs = np.arange(8, dtype=np.float64)
    weights = np.where(freqs == 0.0, math.sqrt(1.0 / 32.0), math.sqrt(2.0 / 32.0))
    return weights[:, None] * np.cos(math.pi * (2.0 * samples[None] + 1.0) * freqs[:, None] / 64.0)


def split(values):
    high = values.astype(ml_dtypes.bfloat16)
    low = (values - high.astype(np.float64)).astype(ml_dtypes.bfloat16)
    return high, low


def tables():
    low = lowband()
    row_high, row_low = split(np.kron(np.eye(ROWS // 32), low))
    col_high, col_low = split(np.kron(np.eye(CHUNK // 32), low.T))
    zero = np.zeros_like(row_high)
    row_enc = np.block([[row_high, row_high], [row_low, zero]])
    col_enc = np.concatenate([col_high, col_low], axis=1)
    row_dec = np.concatenate([row_high.T, row_high.T, row_low.T], axis=1)
    pad = np.zeros((ROWS, 32), ml_dtypes.bfloat16)
    row_dec = np.concatenate([row_dec, pad], axis=1)
    col_dec = np.concatenate([col_high.T, col_high.T, col_low.T], axis=0)
    return row_enc, col_enc, row_dec, col_dec


def dot(a, b):
    return jnp.dot(a, b, preferred_element_type=F32)


def halves(x):
    high = x.astype(BF16)
    return high, (x - high.astype(F32)).astype(BF16)


def encode_kernel(chunks, m_hbm, g_hbm, row_hbm, col_hbm, bands_ref, m, g, row, col, mixed, sems):
    copies = []
    for i in range(chunks):
        cols = pl.ds(i * CHUNK, CHUNK)
        copies.append(
            (
                pltpu.make_async_copy(m_hbm.at[:, cols], m.at[i], sems.at[0, i]),
                pltpu.make_async_copy(g_hbm.at[:, cols], g.at[i], sems.at[1, i]),
            )
        )
    tables_in = (
        pltpu.make_async_copy(row_hbm, row, sems.at[0, chunks]),
        pltpu.make_async_copy(col_hbm, col, sems.at[1, chunks]),
    )
    tables_in[0].start()
    for pair in copies:
        pair[0].start()
        pair[1].start()
    tables_in[1].start()
    tables_in[0].wait()
    for i in range(chunks):
        copies[i][0].wait()
        copies[i][1].wait()
        moment = 0.999 * m[i] + g[i].astype(F32)
        both = dot(row[...], jnp.concatenate(halves(moment), axis=0))
        mixed[pl.ds(i * 32, 32), :] = both[:32] + both[32:]
    tables_in[1].wait()
    high, low = halves(mixed[...])
    first = dot(high, col[...])
    bands_ref[...] = first[:, :128] + first[:, 128:] + dot(low, col[:, :128])


def expand(bands, row, col):
    high, low = halves(bands)
    return dot(jnp.concatenate([high, low, high], axis=1), col)


def rows_of(part, row):
    high, low = halves(part)
    stack = jnp.concatenate([high, low, high, jnp.zeros_like(high)], axis=0)
    return dot(row, stack)


def residual_kernel(chunks, m_hbm, g_hbm, bands_ref, row_ref, col_ref, out_hbm, m, g, spread, sems):
    loads, stores = [], []
    for i in range(chunks):
        cols = pl.ds(i * CHUNK, CHUNK)
        loads.append(
            (
                pltpu.make_async_copy(m_hbm.at[:, cols], m.at[i], sems.at[0, i]),
                pltpu.make_async_copy(g_hbm.at[:, cols], g.at[i], sems.at[1, i]),
            )
        )
        stores.append(pltpu.make_async_copy(m.at[i], out_hbm.at[:, cols], sems.at[2, i]))
    for pair in loads:
        pair[0].start()
        pair[1].start()
    spread[...] = expand(bands_ref[...], row_ref[...], col_ref[...])
    for i in range(chunks):
        loads[i][0].wait()
        loads[i][1].wait()
        moment = 0.999 * m[i] + g[i].astype(F32)
        m[i] = moment - rows_of(spread[pl.ds(i * 32, 32), :], row_ref[...])
        stores[i].start()
    for store in stores:
        store.wait()


def update_kernel(chunks, bands_ref, energy_ref, row_ref, col_ref, out_hbm, out, spread, sems):
    energy = jnp.sum(energy_ref[...])
    scale = lax.rsqrt(jnp.full((1, 128), energy * (1.0 / (ROWS * FF)) + 1e-06, F32))
    spread[...] = expand(bands_ref[...] * scale, row_ref[...], col_ref[...])
    stores = []
    for i in range(chunks):
        cols = pl.ds(i * CHUNK, CHUNK)
        out[i] = rows_of(spread[pl.ds(i * 32, 32), :], row_ref[...])
        stores.append(pltpu.make_async_copy(out.at[i], out_hbm.at[:, cols], sems.at[i]))
        stores[-1].start()
    for store in stores:
        store.wait()


PARAMS = pltpu.CompilerParams(vmem_limit_bytes=24 * 1024 * 1024)


def in_hbm(x):
    return pltpu.with_memory_space_constraint(x, pltpu.HBM)


def encode(m, g, row, col):
    chunks = m.shape[1] // CHUNK
    return pl.pallas_call(
        lambda *refs: encode_kernel(chunks, *refs),
        out_shape=jax.ShapeDtypeStruct((chunks * 32, 128), F32),
        in_specs=[HBM] * 4,
        out_specs=VMEM,
        scratch_shapes=[
            pltpu.VMEM((chunks, ROWS, CHUNK), F32),
            pltpu.VMEM((chunks, ROWS, CHUNK), BF16),
            pltpu.VMEM(row.shape, BF16),
            pltpu.VMEM(col.shape, BF16),
            pltpu.VMEM((chunks * 32, CHUNK), F32),
            pltpu.SemaphoreType.DMA((2, chunks + 1)),
        ],
        compiler_params=PARAMS,
        cost_estimate=pl.CostEstimate(flops=4 * 10**7, bytes_accessed=3 * 10**6, transcendentals=0),
        name="encode",
    )(*(in_hbm(a) for a in (m, g, row, col)))


def residual(m, g, bands, row, col):
    chunks = m.shape[1] // CHUNK
    return pl.pallas_call(
        lambda *refs: residual_kernel(chunks, *refs),
        out_shape=jax.ShapeDtypeStruct(m.shape, F32),
        in_specs=[HBM, HBM, VMEM, VMEM, VMEM],
        out_specs=HBM,
        scratch_shapes=[
            pltpu.VMEM((chunks, ROWS, CHUNK), F32),
            pltpu.VMEM((chunks, ROWS, CHUNK), BF16),
            pltpu.VMEM((chunks * 32, CHUNK), F32),
            pltpu.SemaphoreType.DMA((3, chunks)),
        ],
        compiler_params=PARAMS,
        cost_estimate=pl.CostEstimate(flops=4 * 10**7, bytes_accessed=5 * 10**6, transcendentals=0),
        name="residual",
    )(in_hbm(m), in_hbm(g), bands, row, col)


def decode(bands, energy, row, col):
    chunks = bands.shape[0] // 32
    return pl.pallas_call(
        lambda *refs: update_kernel(chunks, *refs),
        out_shape=jax.ShapeDtypeStruct((ROWS, chunks * CHUNK), F32),
        in_specs=[VMEM] * 4,
        out_specs=HBM,
        scratch_shapes=[
            pltpu.VMEM((chunks, ROWS, CHUNK), F32),
            pltpu.VMEM((chunks * 32, CHUNK), F32),
            pltpu.SemaphoreType.DMA((chunks,)),
        ],
        compiler_params=PARAMS,
        cost_estimate=pl.CostEstimate(flops=4 * 10**7, bytes_accessed=2 * 10**6, transcendentals=0),
        name="decode",
    )(bands, energy, row, col)


def partners(pairs):
    other = {}
    for a, b in pairs:
        other[a], other[b] = b, a
    return other


def along_z(pairs):
    other = partners(pairs)
    return [(8 * x + z, 8 * x + other[z]) for x in range(4) for z in range(8)]


def along_x(pairs):
    other = partners(pairs)
    return [(8 * x + z, 8 * other[x] + z) for x in range(4) for z in range(8)]


EXCHANGES = (
    along_z([(0, 1), (2, 3), (4, 5), (6, 7)]),
    along_z([(1, 2), (3, 4), (5, 6), (7, 0)]),
    along_z([(0, 3), (1, 6), (2, 5), (4, 7)]),
    along_x([(0, 1), (2, 3)]),
    along_x([(1, 2), (3, 0)]),
)


def local(momentum, grad):
    row_enc, col_enc, row_dec, col_dec = (jnp.asarray(t) for t in tables())
    momentum, grad = momentum[0], grad[0]
    bands = encode(momentum, grad, row_enc, col_enc)
    new_momentum = residual(momentum, grad, bands, row_dec, col_dec)
    summed = bands
    for step, pairs in enumerate(EXCHANGES):
        summed = summed + lax.ppermute(summed, "dp", pairs)
        if step == 2:
            summed, new_momentum = lax.optimization_barrier((summed, new_momentum))
    squares = jnp.sum((summed * summed).reshape(-1, 8, 128), axis=0)
    energy = lax.all_to_all(jnp.broadcast_to(squares[None], (8, 8, 128)), "tensor", 0, 0)
    update = decode(summed, energy.reshape(64, 128), row_dec, col_dec)
    return (new_momentum[None], update)


def solution(mesh):
    return jax.shard_map(
        local,
        mesh=mesh,
        in_specs=(P("dp", None, "tensor"), P("dp", None, "tensor")),
        out_specs=(P("dp", None, "tensor"), P(None, "tensor")),
        check_vma=False,
    )
```

```python
import math

import jax
import jax.numpy as jnp
import ml_dtypes
import numpy as np
from jax import lax
from jax.experimental import pallas as pl
from jax.experimental.pallas import tpu as pltpu
from jax.sharding import PartitionSpec as P

FF = 28672
ROWS = 128
CHUNK = 512
F32 = jnp.float32
BF16 = jnp.bfloat16
HBM = pl.BlockSpec(memory_space=pltpu.HBM)
VMEM = pl.BlockSpec(memory_space=pltpu.VMEM)


def lowband():
    samples = np.arange(32, dtype=np.float64)
    freqs = np.arange(8, dtype=np.float64)
    weights = np.where(freqs == 0.0, math.sqrt(1.0 / 32.0), math.sqrt(2.0 / 32.0))
    return weights[:, None] * np.cos(math.pi * (2.0 * samples[None] + 1.0) * freqs[:, None] / 64.0)


def split(values):
    high = values.astype(ml_dtypes.bfloat16)
    low = (values - high.astype(np.float64)).astype(ml_dtypes.bfloat16)
    return high, low


def tables():
    low = lowband()
    row_high, row_low = split(np.kron(np.eye(ROWS // 32), low))
    col_high, col_low = split(np.kron(np.eye(CHUNK // 32), low.T))
    zero = np.zeros_like(row_high)
    row_enc = np.block([[row_high, row_high], [row_low, zero]])
    col_enc = np.concatenate([col_high, col_low], axis=1)
    row_dec = np.concatenate([row_high.T, row_high.T, row_low.T], axis=1)
    pad = np.zeros((ROWS, 32), ml_dtypes.bfloat16)
    row_dec = np.concatenate([row_dec, pad], axis=1)
    col_dec = np.concatenate([col_high.T, col_high.T, col_low.T], axis=0)
    return row_enc, col_enc, row_dec, col_dec


def dot(a, b):
    return jnp.dot(a, b, preferred_element_type=F32)


def halves(x):
    high = x.astype(BF16)
    return high, (x - high.astype(F32)).astype(BF16)


def ordered(first, second):
    odd = lax.rem(lax.axis_index("dp") // 8, 2) == 1
    return jnp.where(odd, second, first), jnp.where(odd, first, second)


def encode_kernel(
    chunks, m_hbm, g_hbm, row_hbm, col_hbm, moment_ref, bands_ref, keep_ref, send_ref, m, g, row, col, mixed, sems
):
    copies = []
    for i in range(chunks):
        cols = pl.ds(i * CHUNK, CHUNK)
        copies.append(
            (
                pltpu.make_async_copy(m_hbm.at[:, cols], m.at[i], sems.at[0, i]),
                pltpu.make_async_copy(g_hbm.at[:, cols], g.at[i], sems.at[1, i]),
            )
        )
    tables_in = (
        pltpu.make_async_copy(row_hbm, row, sems.at[0, chunks]),
        pltpu.make_async_copy(col_hbm, col, sems.at[1, chunks]),
    )
    tables_in[0].start()
    for pair in copies:
        pair[0].start()
        pair[1].start()
    tables_in[1].start()
    tables_in[0].wait()
    for i in range(chunks):
        copies[i][0].wait()
        copies[i][1].wait()
        moment = 0.999 * m[i] + g[i].astype(F32)
        moment_ref[i] = moment
        both = dot(row[...], jnp.concatenate(halves(moment), axis=0))
        mixed[pl.ds(i * 32, 32), :] = both[:32] + both[32:]
    tables_in[1].wait()
    high, low = halves(mixed[...])
    first = dot(high, col[...])
    bands = first[:, :128] + first[:, 128:] + dot(low, col[:, :128])
    bands_ref[...] = bands
    half = bands.shape[0] // 2
    keep_ref[...], send_ref[...] = ordered(bands[:half], bands[half:])


def expand(bands, row, col):
    high, low = halves(bands)
    return dot(jnp.concatenate([high, low, high], axis=1), col)


def rows_of(part, row):
    high, low = halves(part)
    stack = jnp.concatenate([high, low, high, jnp.zeros_like(high)], axis=0)
    return dot(row, stack)


def residual_kernel(chunks, moment_ref, bands_ref, row_ref, col_ref, out_hbm, out, spread, sems):
    spread[...] = expand(bands_ref[...], row_ref[...], col_ref[...])
    stores = []
    for i in range(chunks):
        cols = pl.ds(i * CHUNK, CHUNK)
        out[i] = moment_ref[i] - rows_of(spread[pl.ds(i * 32, 32), :], row_ref[...])
        stores.append(pltpu.make_async_copy(out.at[i], out_hbm.at[:, cols], sems.at[i]))
        stores[-1].start()
    for store in stores:
        store.wait()


def update_kernel(chunks, own_ref, other_ref, energy_ref, row_ref, col_ref, out_hbm, out, spread, sems):
    energy = jnp.sum(energy_ref[...])
    scale = lax.rsqrt(jnp.full((1, 128), energy * (1.0 / (ROWS * FF)) + 1e-06, F32))
    bands = jnp.concatenate(ordered(own_ref[...], other_ref[...]), axis=0)
    spread[...] = expand(bands * scale, row_ref[...], col_ref[...])
    stores = []
    for i in range(chunks):
        cols = pl.ds(i * CHUNK, CHUNK)
        out[i] = rows_of(spread[pl.ds(i * 32, 32), :], row_ref[...])
        stores.append(pltpu.make_async_copy(out.at[i], out_hbm.at[:, cols], sems.at[i]))
        stores[-1].start()
    for store in stores:
        store.wait()


PARAMS = pltpu.CompilerParams(vmem_limit_bytes=24 * 1024 * 1024)


def in_hbm(x):
    return pltpu.with_memory_space_constraint(x, pltpu.HBM)


def encode(m, g, row, col):
    chunks = m.shape[1] // CHUNK
    return pl.pallas_call(
        lambda *refs: encode_kernel(chunks, *refs),
        out_shape=[jax.ShapeDtypeStruct((chunks, ROWS, CHUNK), F32)]
        + [jax.ShapeDtypeStruct((rows, 128), F32) for rows in (chunks * 32, chunks * 16, chunks * 16)],
        in_specs=[HBM] * 4,
        out_specs=[VMEM] * 4,
        scratch_shapes=[
            pltpu.VMEM((chunks, ROWS, CHUNK), F32),
            pltpu.VMEM((chunks, ROWS, CHUNK), BF16),
            pltpu.VMEM(row.shape, BF16),
            pltpu.VMEM(col.shape, BF16),
            pltpu.VMEM((chunks * 32, CHUNK), F32),
            pltpu.SemaphoreType.DMA((2, chunks + 1)),
        ],
        compiler_params=PARAMS,
        cost_estimate=pl.CostEstimate(flops=4 * 10**7, bytes_accessed=3 * 10**6, transcendentals=0),
        name="encode",
    )(*(in_hbm(a) for a in (m, g, row, col)))


def residual(moment, bands, row, col):
    chunks = moment.shape[0]
    return pl.pallas_call(
        lambda *refs: residual_kernel(chunks, *refs),
        out_shape=jax.ShapeDtypeStruct((ROWS, chunks * CHUNK), F32),
        in_specs=[VMEM] * 4,
        out_specs=HBM,
        scratch_shapes=[
            pltpu.VMEM((chunks, ROWS, CHUNK), F32),
            pltpu.VMEM((chunks * 32, CHUNK), F32),
            pltpu.SemaphoreType.DMA((chunks,)),
        ],
        compiler_params=PARAMS,
        cost_estimate=pl.CostEstimate(flops=4 * 10**7, bytes_accessed=5 * 10**6, transcendentals=0),
        name="residual",
    )(moment, bands, row, col)


def decode(own, other, energy, row, col):
    chunks = own.shape[0] // 16
    return pl.pallas_call(
        lambda *refs: update_kernel(chunks, *refs),
        out_shape=jax.ShapeDtypeStruct((ROWS, chunks * CHUNK), F32),
        in_specs=[VMEM] * 5,
        out_specs=HBM,
        scratch_shapes=[
            pltpu.VMEM((chunks, ROWS, CHUNK), F32),
            pltpu.VMEM((chunks * 32, CHUNK), F32),
            pltpu.SemaphoreType.DMA((chunks,)),
        ],
        compiler_params=PARAMS,
        cost_estimate=pl.CostEstimate(flops=4 * 10**7, bytes_accessed=2 * 10**6, transcendentals=0),
        name="decode",
    )(own, other, energy, row, col)


def partners(pairs):
    other = {}
    for a, b in pairs:
        other[a], other[b] = b, a
    return other


def along_z(pairs):
    other = partners(pairs)
    return [(8 * x + z, 8 * x + other[z]) for x in range(4) for z in range(8)]


def along_x(pairs):
    other = partners(pairs)
    return [(8 * x + z, 8 * other[x] + z) for x in range(4) for z in range(8)]


HALVES = along_x([(0, 1), (2, 3)])
STEPS = (
    (
        along_z([(0, 3), (1, 2), (4, 7), (5, 6)]),
        along_z([(0, 2), (1, 3), (4, 6), (5, 7)]),
        along_z([(0, 1), (2, 3), (4, 5), (6, 7)]),
    ),
    (along_z([(0, 7), (1, 6), (2, 5), (3, 4)]),),
)
BOTH = [
    [(8 * x + z) * 8 + t for x in pair for t in range(8)] for pair in ((0, 1), (2, 3)) for z in range(8)
]


def local(momentum, grad):
    row_enc, col_enc, row_dec, col_dec = (jnp.asarray(t) for t in tables())
    momentum, grad = momentum[0], grad[0]
    moment, bands, keep, send = encode(momentum, grad, row_enc, col_enc)
    new_momentum = residual(moment, bands, row_dec, col_dec)
    own = (
        keep
        + lax.ppermute(keep, "dp", along_x([(0, 2), (1, 3)]))
        + lax.ppermute(send, "dp", along_x([(1, 2), (3, 0)]))
        + lax.ppermute(send, "dp", HALVES)
    )
    for step in STEPS:
        own = sum((lax.ppermute(own, "dp", pairs) for pairs in step), own)
    other = lax.ppermute(own, "dp", HALVES)
    squares = jnp.sum((own * own).reshape(-1, 8, 128), axis=0)
    energy = lax.all_to_all(
        jnp.broadcast_to(squares[None], (16, 8, 128)), ("dp", "tensor"), 0, 0, axis_index_groups=BOTH
    )
    update = decode(own, other, energy.reshape(128, 128), row_dec, col_dec)
    return (new_momentum[None], update)


def solution(mesh):
    return jax.shard_map(
        local,
        mesh=mesh,
        in_specs=(P("dp", None, "tensor"), P("dp", None, "tensor")),
        out_specs=(P("dp", None, "tensor"), P(None, "tensor")),
        check_vma=False,
    )
```

```python
import math

import jax
import jax.numpy as jnp
import ml_dtypes
import numpy as np
from jax import lax
from jax.experimental import pallas as pl
from jax.experimental.pallas import tpu as pltpu
from jax.sharding import PartitionSpec as P

FF = 28672
ROWS = 128
CHUNK = 512
F32 = jnp.float32
BF16 = jnp.bfloat16
HBM = pl.BlockSpec(memory_space=pltpu.HBM)
VMEM = pl.BlockSpec(memory_space=pltpu.VMEM)


def lowband():
    samples = np.arange(32, dtype=np.float64)
    freqs = np.arange(8, dtype=np.float64)
    weights = np.where(freqs == 0.0, math.sqrt(1.0 / 32.0), math.sqrt(2.0 / 32.0))
    return weights[:, None] * np.cos(math.pi * (2.0 * samples[None] + 1.0) * freqs[:, None] / 64.0)


def split(values):
    high = values.astype(ml_dtypes.bfloat16)
    low = (values - high.astype(np.float64)).astype(ml_dtypes.bfloat16)
    return high, low


def tables():
    low = lowband()
    row_high, row_low = split(np.kron(np.eye(ROWS // 32), low))
    col_high, col_low = split(np.kron(np.eye(CHUNK // 32), low.T))
    zero = np.zeros_like(row_high)
    row_enc = np.block([[row_high, row_high], [row_low, zero]])
    col_enc = np.concatenate([col_high, col_low], axis=1)
    row_dec = np.concatenate([row_high.T, row_high.T, row_low.T], axis=1)
    pad = np.zeros((ROWS, 32), ml_dtypes.bfloat16)
    row_dec = np.concatenate([row_dec, pad], axis=1)
    col_dec = np.concatenate([col_high.T, col_high.T, col_low.T], axis=0)
    return row_enc, col_enc, row_dec, col_dec


def dot(a, b):
    return jnp.dot(a, b, preferred_element_type=F32)


def halves(x):
    high = x.astype(BF16)
    return high, (x - high.astype(F32)).astype(BF16)


def ordered(first, second):
    odd = lax.rem(lax.axis_index("dp") // 8, 2) == 1
    return jnp.where(odd, second, first), jnp.where(odd, first, second)


def encode_kernel(
    chunks, m_hbm, g_hbm, row_hbm, col_hbm, moment_ref, bands_ref, keep_ref, send_ref, m, g, row, col, mixed, sems
):
    copies = []
    for i in range(chunks):
        cols = pl.ds(i * CHUNK, CHUNK)
        copies.append(
            (
                pltpu.make_async_copy(m_hbm.at[:, cols], m.at[i], sems.at[0, i]),
                pltpu.make_async_copy(g_hbm.at[:, cols], g.at[i], sems.at[1, i]),
            )
        )
    tables_in = (
        pltpu.make_async_copy(row_hbm, row, sems.at[0, chunks]),
        pltpu.make_async_copy(col_hbm, col, sems.at[1, chunks]),
    )
    tables_in[0].start()
    for pair in copies:
        pair[0].start()
        pair[1].start()
    tables_in[1].start()
    tables_in[0].wait()
    for group in (range(1), range(1, chunks // 2 + 1), range(chunks // 2 + 1, chunks)):
        for i in group:
            copies[i][0].wait()
            copies[i][1].wait()
        for i in group:
            moment = 0.999 * m[i] + g[i].astype(F32)
            moment_ref[i] = moment
            both = dot(row[...], jnp.concatenate(halves(moment), axis=0))
            mixed[pl.ds(i * 32, 32), :] = both[:32] + both[32:]
    tables_in[1].wait()
    high, low = halves(mixed[...])
    first = dot(high, col[...])
    bands = first[:, :128] + first[:, 128:] + dot(low, col[:, :128])
    bands_ref[...] = bands
    half = bands.shape[0] // 2
    keep_ref[...], send_ref[...] = ordered(bands[:half], bands[half:])


def expand(bands, col):
    high, low = halves(bands)
    return dot(jnp.concatenate([high, low, high], axis=1), col)


def stacked(part):
    high, low = halves(part)
    return jnp.concatenate([high, low, high, jnp.zeros_like(high)], axis=0)


def rows_of(part, row):
    return dot(row, stacked(part))


def residual_kernel(chunks, moment_ref, bands_ref, row_ref, col_ref, out_hbm, out, spread, sems):
    spread[...] = expand(bands_ref[...], col_ref[...])
    stores = []
    for i in range(chunks):
        cols = pl.ds(i * CHUNK, CHUNK)
        out[i] = moment_ref[i] - rows_of(spread[pl.ds(i * 32, 32), :], row_ref[...])
        stores.append(pltpu.make_async_copy(out.at[i], out_hbm.at[:, cols], sems.at[i]))
        stores[-1].start()
    for store in stores:
        store.wait()


def spread_kernel(chunks, own_ref, other_ref, col_ref, stack_ref):
    bands = jnp.concatenate(ordered(own_ref[...], other_ref[...]), axis=0)
    mixed = expand(bands, col_ref[...])
    for i in range(chunks):
        stack_ref[i] = stacked(mixed[i * 32 : (i + 1) * 32])


def update_kernel(chunks, stack_ref, energy_ref, row_ref, out_hbm, out, sems):
    energy = jnp.sum(energy_ref[...])
    scale = lax.rsqrt(jnp.full((1, CHUNK), energy * (1.0 / (ROWS * FF)) + 1e-06, F32))
    stores = []
    for i in range(chunks):
        cols = pl.ds(i * CHUNK, CHUNK)
        out[i] = dot(row_ref[...], stack_ref[i]) * scale
        stores.append(pltpu.make_async_copy(out.at[i], out_hbm.at[:, cols], sems.at[i]))
        stores[-1].start()
    for store in stores:
        store.wait()


PARAMS = pltpu.CompilerParams(vmem_limit_bytes=24 * 1024 * 1024)


def in_hbm(x):
    return pltpu.with_memory_space_constraint(x, pltpu.HBM)


def encode(m, g, row, col):
    chunks = m.shape[1] // CHUNK
    return pl.pallas_call(
        lambda *refs: encode_kernel(chunks, *refs),
        out_shape=[jax.ShapeDtypeStruct((chunks, ROWS, CHUNK), F32)]
        + [jax.ShapeDtypeStruct((rows, 128), F32) for rows in (chunks * 32, chunks * 16, chunks * 16)],
        in_specs=[HBM] * 4,
        out_specs=[VMEM] * 4,
        scratch_shapes=[
            pltpu.VMEM((chunks, ROWS, CHUNK), F32),
            pltpu.VMEM((chunks, ROWS, CHUNK), BF16),
            pltpu.VMEM(row.shape, BF16),
            pltpu.VMEM(col.shape, BF16),
            pltpu.VMEM((chunks * 32, CHUNK), F32),
            pltpu.SemaphoreType.DMA((2, chunks + 1)),
        ],
        compiler_params=PARAMS,
        cost_estimate=pl.CostEstimate(flops=4 * 10**7, bytes_accessed=3 * 10**6, transcendentals=0),
        name="encode",
    )(*(in_hbm(a) for a in (m, g, row, col)))


def residual(moment, bands, row, col):
    chunks = moment.shape[0]
    return pl.pallas_call(
        lambda *refs: residual_kernel(chunks, *refs),
        out_shape=jax.ShapeDtypeStruct((ROWS, chunks * CHUNK), F32),
        in_specs=[VMEM] * 4,
        out_specs=HBM,
        scratch_shapes=[
            pltpu.VMEM((chunks, ROWS, CHUNK), F32),
            pltpu.VMEM((chunks * 32, CHUNK), F32),
            pltpu.SemaphoreType.DMA((chunks,)),
        ],
        compiler_params=PARAMS,
        cost_estimate=pl.CostEstimate(flops=4 * 10**7, bytes_accessed=5 * 10**6, transcendentals=0),
        name="residual",
    )(moment, bands, row, col)


def spread(own, other, col):
    chunks = own.shape[0] // 16
    return pl.pallas_call(
        lambda *refs: spread_kernel(chunks, *refs),
        out_shape=jax.ShapeDtypeStruct((chunks, 128, CHUNK), BF16),
        in_specs=[VMEM] * 3,
        out_specs=VMEM,
        compiler_params=PARAMS,
        cost_estimate=pl.CostEstimate(flops=4 * 10**7, bytes_accessed=10**6, transcendentals=0),
        name="spread",
    )(own, other, col)


def decode(stack, energy, row):
    chunks = stack.shape[0]
    return pl.pallas_call(
        lambda *refs: update_kernel(chunks, *refs),
        out_shape=jax.ShapeDtypeStruct((ROWS, chunks * CHUNK), F32),
        in_specs=[VMEM] * 3,
        out_specs=HBM,
        scratch_shapes=[
            pltpu.VMEM((chunks, ROWS, CHUNK), F32),
            pltpu.SemaphoreType.DMA((chunks,)),
        ],
        compiler_params=PARAMS,
        cost_estimate=pl.CostEstimate(flops=4 * 10**7, bytes_accessed=2 * 10**6, transcendentals=0),
        name="decode",
    )(stack, energy, row)


def partners(pairs):
    other = {}
    for a, b in pairs:
        other[a], other[b] = b, a
    return other


def along_z(pairs):
    other = partners(pairs)
    return [(8 * x + z, 8 * x + other[z]) for x in range(4) for z in range(8)]


def along_x(pairs):
    other = partners(pairs)
    return [(8 * x + z, 8 * other[x] + z) for x in range(4) for z in range(8)]


HALVES = along_x([(0, 1), (2, 3)])
STEPS = (
    (
        along_z([(0, 3), (1, 2), (4, 7), (5, 6)]),
        along_z([(0, 2), (1, 3), (4, 6), (5, 7)]),
        along_z([(0, 1), (2, 3), (4, 5), (6, 7)]),
    ),
    (along_z([(0, 7), (1, 6), (2, 5), (3, 4)]),),
)
BOTH = [
    [(8 * x + z) * 8 + t for x in pair for t in range(8)] for pair in ((0, 1), (2, 3)) for z in range(8)
]


def local(momentum, grad):
    row_enc, col_enc, row_dec, col_dec = (jnp.asarray(t) for t in tables())
    momentum, grad = momentum[0], grad[0]
    moment, bands, keep, send = encode(momentum, grad, row_enc, col_enc)
    new_momentum = residual(moment, bands, row_dec, col_dec)
    own = (
        keep
        + lax.ppermute(keep, "dp", along_x([(0, 2), (1, 3)]))
        + lax.ppermute(send, "dp", along_x([(1, 2), (3, 0)]))
        + lax.ppermute(send, "dp", HALVES)
    )
    for step in STEPS:
        own = sum((lax.ppermute(own, "dp", pairs) for pairs in step), own)
    own, new_momentum = lax.optimization_barrier((own, new_momentum))
    other = lax.ppermute(own, "dp", HALVES)
    squares = jnp.sum((own * own).reshape(-1, 8, 128), axis=0)
    energy = lax.all_to_all(
        jnp.broadcast_to(squares[None], (16, 8, 128)), ("dp", "tensor"), 0, 0, axis_index_groups=BOTH
    )
    update = decode(spread(own, other, col_dec), energy.reshape(128, 128), row_dec)
    return (new_momentum[None], update)


def solution(mesh):
    return jax.shard_map(
        local,
        mesh=mesh,
        in_specs=(P("dp", None, "tensor"), P("dp", None, "tensor")),
        out_specs=(P("dp", None, "tensor"), P(None, "tensor")),
        check_vma=False,
    )
```

```python
import math

import jax
import jax.numpy as jnp
import ml_dtypes
import numpy as np
from jax import lax
from jax.experimental import pallas as pl
from jax.experimental.pallas import tpu as pltpu
from jax.sharding import PartitionSpec as P

FF = 28672
ROWS = 128
CHUNK = 512
F32 = jnp.float32
BF16 = jnp.bfloat16
HBM = pl.BlockSpec(memory_space=pltpu.HBM)
VMEM = pl.BlockSpec(memory_space=pltpu.VMEM)


def lowband():
    samples = np.arange(32, dtype=np.float64)
    freqs = np.arange(8, dtype=np.float64)
    weights = np.where(freqs == 0.0, math.sqrt(1.0 / 32.0), math.sqrt(2.0 / 32.0))
    return weights[:, None] * np.cos(math.pi * (2.0 * samples[None] + 1.0) * freqs[:, None] / 64.0)


def split(values):
    high = values.astype(ml_dtypes.bfloat16)
    low = (values - high.astype(np.float64)).astype(ml_dtypes.bfloat16)
    return high, low


def tables():
    low = lowband()
    row_high, row_low = split(np.kron(np.eye(ROWS // 32), low))
    col_high, col_low = split(np.kron(np.eye(CHUNK // 32), low.T))
    zero = np.zeros_like(row_high)
    row_enc = np.block([[row_high, row_high], [row_low, zero]])
    col_enc = np.concatenate([col_high, col_low], axis=1)
    row_dec = np.concatenate([row_high.T, row_high.T, row_low.T], axis=1)
    pad = np.zeros((ROWS, 32), ml_dtypes.bfloat16)
    row_dec = np.concatenate([row_dec, pad], axis=1)
    col_dec = np.concatenate([col_high.T, col_high.T, col_low.T], axis=0)
    return row_enc, col_enc, row_dec, col_dec


def dot(a, b):
    return jnp.dot(a, b, preferred_element_type=F32)


def halves(x):
    high = x.astype(BF16)
    return high, (x - high.astype(F32)).astype(BF16)


def ordered(first, second):
    odd = lax.rem(lax.axis_index("dp") // 8, 2) == 1
    return jnp.where(odd, second, first), jnp.where(odd, first, second)


def encode_kernel(
    chunks, m_hbm, g_hbm, row_hbm, col_hbm, moment_ref, bands_ref, keep_ref, send_ref, m, g, row, col, mixed, sems
):
    copies = []
    for i in range(chunks):
        cols = pl.ds(i * CHUNK, CHUNK)
        copies.append(
            (
                pltpu.make_async_copy(m_hbm.at[:, cols], m.at[i], sems.at[0, i]),
                pltpu.make_async_copy(g_hbm.at[:, cols], g.at[i], sems.at[1, i]),
            )
        )
    tables_in = (
        pltpu.make_async_copy(row_hbm, row, sems.at[0, chunks]),
        pltpu.make_async_copy(col_hbm, col, sems.at[1, chunks]),
    )
    tables_in[0].start()
    for pair in copies:
        pair[0].start()
        pair[1].start()
    tables_in[1].start()
    tables_in[0].wait()
    for group in (range(1), range(1, chunks // 2 + 1), range(chunks // 2 + 1, chunks)):
        for i in group:
            copies[i][0].wait()
            copies[i][1].wait()
        for i in group:
            moment = 0.999 * m[i] + g[i].astype(F32)
            moment_ref[i] = moment
            both = dot(row[...], jnp.concatenate(halves(moment), axis=0))
            mixed[pl.ds(i * 32, 32), :] = both[:32] + both[32:]
    tables_in[1].wait()
    high, low = halves(mixed[...])
    first = dot(high, col[...])
    bands = first[:, :128] + first[:, 128:] + dot(low, col[:, :128])
    bands_ref[...] = bands
    half = bands.shape[0] // 2
    keep_ref[...], send_ref[...] = ordered(bands[:half], bands[half:])


def expand(bands, col):
    high, low = halves(bands)
    return dot(jnp.concatenate([high, low, high], axis=1), col)


def stacked(part):
    high, low = halves(part)
    return jnp.concatenate([high, low, high, jnp.zeros_like(high)], axis=0)


def rows_of(part, row):
    return dot(row, stacked(part))


def residual_kernel(chunks, moment_ref, bands_ref, row_ref, col_ref, out_hbm, out, spread, sems):
    spread[...] = expand(bands_ref[...], col_ref[...])
    stores = []
    for i in range(chunks):
        cols = pl.ds(i * CHUNK, CHUNK)
        out[i] = moment_ref[i] - rows_of(spread[pl.ds(i * 32, 32), :], row_ref[...])
        stores.append(pltpu.make_async_copy(out.at[i], out_hbm.at[:, cols], sems.at[i]))
        stores[-1].start()
    for store in stores:
        store.wait()


def spread_kernel(chunks, own_ref, other_ref, col_ref, stack_ref):
    bands = jnp.concatenate(ordered(own_ref[...], other_ref[...]), axis=0)
    mixed = expand(bands, col_ref[...])
    for i in range(chunks):
        stack_ref[i] = stacked(mixed[i * 32 : (i + 1) * 32])


def update_kernel(chunks, stack_ref, energy_ref, row_ref, out_hbm, out, sems):
    energy = jnp.sum(energy_ref[...])
    scale = lax.rsqrt(jnp.full((1, CHUNK), energy * (1.0 / (ROWS * FF)) + 1e-06, F32))
    stores = []
    for i in range(chunks):
        cols = pl.ds(i * CHUNK, CHUNK)
        out[i] = dot(row_ref[...], stack_ref[i]) * scale
        stores.append(pltpu.make_async_copy(out.at[i], out_hbm.at[:, cols], sems.at[i]))
        stores[-1].start()
    for store in stores:
        store.wait()


PARAMS = pltpu.CompilerParams(vmem_limit_bytes=24 * 1024 * 1024)


def in_hbm(x):
    return pltpu.with_memory_space_constraint(x, pltpu.HBM)


def encode(m, g, row, col):
    chunks = m.shape[1] // CHUNK
    return pl.pallas_call(
        lambda *refs: encode_kernel(chunks, *refs),
        out_shape=[jax.ShapeDtypeStruct((chunks, ROWS, CHUNK), F32)]
        + [jax.ShapeDtypeStruct((rows, 128), F32) for rows in (chunks * 32, chunks * 16, chunks * 16)],
        in_specs=[HBM] * 4,
        out_specs=[VMEM] * 4,
        scratch_shapes=[
            pltpu.VMEM((chunks, ROWS, CHUNK), F32),
            pltpu.VMEM((chunks, ROWS, CHUNK), BF16),
            pltpu.VMEM(row.shape, BF16),
            pltpu.VMEM(col.shape, BF16),
            pltpu.VMEM((chunks * 32, CHUNK), F32),
            pltpu.SemaphoreType.DMA((2, chunks + 1)),
        ],
        compiler_params=PARAMS,
        cost_estimate=pl.CostEstimate(flops=4 * 10**7, bytes_accessed=3 * 10**6, transcendentals=0),
        name="encode",
    )(*(in_hbm(a) for a in (m, g, row, col)))


def residual(moment, bands, row, col):
    chunks = moment.shape[0]
    return pl.pallas_call(
        lambda *refs: residual_kernel(chunks, *refs),
        out_shape=jax.ShapeDtypeStruct((ROWS, chunks * CHUNK), F32),
        in_specs=[VMEM] * 4,
        out_specs=HBM,
        scratch_shapes=[
            pltpu.VMEM((chunks, ROWS, CHUNK), F32),
            pltpu.VMEM((chunks * 32, CHUNK), F32),
            pltpu.SemaphoreType.DMA((chunks,)),
        ],
        compiler_params=PARAMS,
        cost_estimate=pl.CostEstimate(flops=4 * 10**7, bytes_accessed=5 * 10**6, transcendentals=0),
        name="residual",
    )(moment, bands, row, col)


def spread(own, other, col):
    chunks = own.shape[0] // 16
    return pl.pallas_call(
        lambda *refs: spread_kernel(chunks, *refs),
        out_shape=jax.ShapeDtypeStruct((chunks, 128, CHUNK), BF16),
        in_specs=[VMEM] * 3,
        out_specs=VMEM,
        compiler_params=PARAMS,
        cost_estimate=pl.CostEstimate(flops=4 * 10**7, bytes_accessed=10**6, transcendentals=0),
        name="spread",
    )(own, other, col)


def decode(stack, energy, row):
    chunks = stack.shape[0]
    return pl.pallas_call(
        lambda *refs: update_kernel(chunks, *refs),
        out_shape=jax.ShapeDtypeStruct((ROWS, chunks * CHUNK), F32),
        in_specs=[VMEM] * 3,
        out_specs=HBM,
        scratch_shapes=[
            pltpu.VMEM((chunks, ROWS, CHUNK), F32),
            pltpu.SemaphoreType.DMA((chunks,)),
        ],
        compiler_params=PARAMS,
        cost_estimate=pl.CostEstimate(flops=4 * 10**7, bytes_accessed=2 * 10**6, transcendentals=0),
        name="decode",
    )(stack, energy, row)


def partners(pairs):
    other = {}
    for a, b in pairs:
        other[a], other[b] = b, a
    return other


def along_z(pairs):
    other = partners(pairs)
    return [(8 * x + z, 8 * x + other[z]) for x in range(4) for z in range(8)]


def along_x(pairs):
    other = partners(pairs)
    return [(8 * x + z, 8 * other[x] + z) for x in range(4) for z in range(8)]


HALVES = along_x([(0, 1), (2, 3)])
STEPS = (
    (
        along_z([(0, 1), (2, 3), (4, 5), (6, 7)]),
        along_z([(0, 2), (1, 3), (4, 6), (5, 7)]),
        along_z([(0, 3), (1, 2), (4, 7), (5, 6)]),
    ),
    (along_z([(0, 7), (1, 6), (2, 5), (3, 4)]),),
)
BOTH = [
    [(8 * x + z) * 8 + t for x in pair for t in range(8)] for pair in ((0, 1), (2, 3)) for z in range(8)
]


def local(momentum, grad):
    row_enc, col_enc, row_dec, col_dec = (jnp.asarray(t) for t in tables())
    momentum, grad = momentum[0], grad[0]
    moment, bands, keep, send = encode(momentum, grad, row_enc, col_enc)
    new_momentum = residual(moment, bands, row_dec, col_dec)
    own = (
        keep
        + lax.ppermute(send, "dp", HALVES)
        + lax.ppermute(send, "dp", along_x([(1, 2), (3, 0)]))
        + lax.ppermute(keep, "dp", along_x([(0, 2), (1, 3)]))
    )
    for step in STEPS:
        own = sum((lax.ppermute(own, "dp", pairs) for pairs in step), own)
    own, new_momentum = lax.optimization_barrier((own, new_momentum))
    other = lax.ppermute(own, "dp", HALVES)
    squares = jnp.sum((own * own).reshape(-1, 8, 128), axis=0)
    energy = lax.all_to_all(
        jnp.broadcast_to(squares[None], (16, 8, 128)), ("dp", "tensor"), 0, 0, axis_index_groups=BOTH
    )
    update = decode(spread(own, other, col_dec), energy.reshape(128, 128), row_dec)
    return (new_momentum[None], update)


def solution(mesh):
    return jax.shard_map(
        local,
        mesh=mesh,
        in_specs=(P("dp", None, "tensor"), P("dp", None, "tensor")),
        out_specs=(P("dp", None, "tensor"), P(None, "tensor")),
        check_vma=False,
    )
```

```python
import math

import jax
import jax.numpy as jnp
import ml_dtypes
import numpy as np
from jax import lax
from jax.experimental import pallas as pl
from jax.experimental.pallas import tpu as pltpu
from jax.sharding import PartitionSpec as P

FF = 28672
ROWS = 128
CHUNK = 512
F32 = jnp.float32
BF16 = jnp.bfloat16
HBM = pl.BlockSpec(memory_space=pltpu.HBM)
VMEM = pl.BlockSpec(memory_space=pltpu.VMEM)


def lowband():
    samples = np.arange(32, dtype=np.float64)
    freqs = np.arange(8, dtype=np.float64)
    weights = np.where(freqs == 0.0, math.sqrt(1.0 / 32.0), math.sqrt(2.0 / 32.0))
    return weights[:, None] * np.cos(math.pi * (2.0 * samples[None] + 1.0) * freqs[:, None] / 64.0)


def split(values):
    high = values.astype(ml_dtypes.bfloat16)
    low = (values - high.astype(np.float64)).astype(ml_dtypes.bfloat16)
    return high, low


def tables():
    low = lowband()
    row_high, row_low = split(np.kron(np.eye(ROWS // 32), low))
    col_high, col_low = split(np.kron(np.eye(CHUNK // 32), low.T))
    zero = np.zeros_like(row_high)
    row_enc = np.block([[row_high, row_high], [row_low, zero]])
    col_enc = np.concatenate([col_high, col_low], axis=1)
    row_dec = np.concatenate([row_high.T, row_high.T, row_low.T], axis=1)
    pad = np.zeros((ROWS, 32), ml_dtypes.bfloat16)
    row_dec = np.concatenate([row_dec, pad], axis=1)
    col_dec = np.concatenate([col_high.T, col_high.T, col_low.T], axis=0)
    return row_enc, col_enc, row_dec, col_dec


def dot(a, b):
    return jnp.dot(a, b, preferred_element_type=F32)


def halves(x):
    high = x.astype(BF16)
    return high, (x - high.astype(F32)).astype(BF16)


def ordered(first, second):
    odd = lax.rem(lax.axis_index("dp") // 8, 2) == 1
    return jnp.where(odd, second, first), jnp.where(odd, first, second)


def encode_kernel(
    chunks, m_hbm, g_hbm, row_hbm, col_hbm, moment_ref, bands_ref, keep_ref, send_ref, m, g, row, col, mixed, sems
):
    copies = []
    for i in range(chunks):
        cols = pl.ds(i * CHUNK, CHUNK)
        copies.append(
            (
                pltpu.make_async_copy(m_hbm.at[:, cols], m.at[i], sems.at[0, i]),
                pltpu.make_async_copy(g_hbm.at[:, cols], g.at[i], sems.at[1, i]),
            )
        )
    tables_in = (
        pltpu.make_async_copy(row_hbm, row, sems.at[0, chunks]),
        pltpu.make_async_copy(col_hbm, col, sems.at[1, chunks]),
    )
    tables_in[0].start()
    for pair in copies:
        pair[0].start()
        pair[1].start()
    tables_in[1].start()
    tables_in[0].wait()
    for group in (range(1), range(1, chunks // 2 + 1), range(chunks // 2 + 1, chunks)):
        for i in group:
            copies[i][0].wait()
            copies[i][1].wait()
        for i in group:
            moment = 0.999 * m[i] + g[i].astype(F32)
            moment_ref[i] = moment
            both = dot(row[...], jnp.concatenate(halves(moment), axis=0))
            mixed[pl.ds(i * 32, 32), :] = both[:32] + both[32:]
    tables_in[1].wait()
    high, low = halves(mixed[...])
    first = dot(high, col[...])
    bands = first[:, :128] + first[:, 128:] + dot(low, col[:, :128])
    bands_ref[...] = bands
    half = bands.shape[0] // 2
    keep_ref[...], send_ref[...] = ordered(bands[:half], bands[half:])


def expand(bands, col):
    high, low = halves(bands)
    return dot(jnp.concatenate([high, low, high], axis=1), col)


def stacked(part):
    high, low = halves(part)
    return jnp.concatenate([high, low, high, jnp.zeros_like(high)], axis=0)


def rows_of(part, row):
    return dot(row, stacked(part))


def residual_kernel(chunks, moment_ref, bands_ref, row_ref, col_ref, out_hbm, out, spread, sems):
    spread[...] = expand(bands_ref[...], col_ref[...])
    stores = []
    for i in range(chunks):
        cols = pl.ds(i * CHUNK, CHUNK)
        out[i] = moment_ref[i] - rows_of(spread[pl.ds(i * 32, 32), :], row_ref[...])
        stores.append(pltpu.make_async_copy(out.at[i], out_hbm.at[:, cols], sems.at[i]))
        stores[-1].start()
    for store in stores:
        store.wait()


def spread_kernel(chunks, own_ref, other_ref, col_ref, stack_ref):
    bands = jnp.concatenate(ordered(own_ref[...], other_ref[...]), axis=0)
    mixed = expand(bands, col_ref[...])
    for i in range(chunks):
        stack_ref[i] = stacked(mixed[i * 32 : (i + 1) * 32])


def update_kernel(chunks, stack_ref, energy_ref, row_ref, out_hbm, out, sems):
    energy = jnp.sum(energy_ref[...])
    scale = lax.rsqrt(jnp.full((1, CHUNK), energy * (1.0 / (ROWS * FF)) + 1e-06, F32))
    stores = []
    for i in range(chunks):
        cols = pl.ds(i * CHUNK, CHUNK)
        out[i] = dot(row_ref[...], stack_ref[i]) * scale
        stores.append(pltpu.make_async_copy(out.at[i], out_hbm.at[:, cols], sems.at[i]))
        stores[-1].start()
    for store in stores:
        store.wait()


PARAMS = pltpu.CompilerParams(vmem_limit_bytes=24 * 1024 * 1024)


def in_hbm(x):
    return pltpu.with_memory_space_constraint(x, pltpu.HBM)


def encode(m, g, row, col):
    chunks = m.shape[1] // CHUNK
    return pl.pallas_call(
        lambda *refs: encode_kernel(chunks, *refs),
        out_shape=[jax.ShapeDtypeStruct((chunks, ROWS, CHUNK), F32)]
        + [jax.ShapeDtypeStruct((rows, 128), F32) for rows in (chunks * 32, chunks * 16, chunks * 16)],
        in_specs=[HBM] * 4,
        out_specs=[VMEM] * 4,
        scratch_shapes=[
            pltpu.VMEM((chunks, ROWS, CHUNK), F32),
            pltpu.VMEM((chunks, ROWS, CHUNK), BF16),
            pltpu.VMEM(row.shape, BF16),
            pltpu.VMEM(col.shape, BF16),
            pltpu.VMEM((chunks * 32, CHUNK), F32),
            pltpu.SemaphoreType.DMA((2, chunks + 1)),
        ],
        compiler_params=PARAMS,
        cost_estimate=pl.CostEstimate(flops=4 * 10**7, bytes_accessed=3 * 10**6, transcendentals=0),
        name="encode",
    )(*(in_hbm(a) for a in (m, g, row, col)))


def residual(moment, bands, row, col):
    chunks = moment.shape[0]
    return pl.pallas_call(
        lambda *refs: residual_kernel(chunks, *refs),
        out_shape=jax.ShapeDtypeStruct((ROWS, chunks * CHUNK), F32),
        in_specs=[VMEM] * 4,
        out_specs=HBM,
        scratch_shapes=[
            pltpu.VMEM((chunks, ROWS, CHUNK), F32),
            pltpu.VMEM((chunks * 32, CHUNK), F32),
            pltpu.SemaphoreType.DMA((chunks,)),
        ],
        compiler_params=PARAMS,
        cost_estimate=pl.CostEstimate(flops=4 * 10**7, bytes_accessed=5 * 10**6, transcendentals=0),
        name="residual",
    )(moment, bands, row, col)


def spread(own, other, col):
    chunks = own.shape[0] // 16
    return pl.pallas_call(
        lambda *refs: spread_kernel(chunks, *refs),
        out_shape=jax.ShapeDtypeStruct((chunks, 128, CHUNK), BF16),
        in_specs=[VMEM] * 3,
        out_specs=VMEM,
        compiler_params=PARAMS,
        cost_estimate=pl.CostEstimate(flops=4 * 10**7, bytes_accessed=10**6, transcendentals=0),
        name="spread",
    )(own, other, col)


def decode(stack, energy, row):
    chunks = stack.shape[0]
    return pl.pallas_call(
        lambda *refs: update_kernel(chunks, *refs),
        out_shape=jax.ShapeDtypeStruct((ROWS, chunks * CHUNK), F32),
        in_specs=[VMEM] * 3,
        out_specs=HBM,
        scratch_shapes=[
            pltpu.VMEM((chunks, ROWS, CHUNK), F32),
            pltpu.SemaphoreType.DMA((chunks,)),
        ],
        compiler_params=PARAMS,
        cost_estimate=pl.CostEstimate(flops=4 * 10**7, bytes_accessed=2 * 10**6, transcendentals=0),
        name="decode",
    )(stack, energy, row)


def partners(pairs):
    other = {}
    for a, b in pairs:
        other[a], other[b] = b, a
    return other


def along_z(pairs):
    other = partners(pairs)
    return [(8 * x + z, 8 * x + other[z]) for x in range(4) for z in range(8)]


def along_x(pairs):
    other = partners(pairs)
    return [(8 * x + z, 8 * other[x] + z) for x in range(4) for z in range(8)]


HALVES = along_x([(0, 1), (2, 3)])
STEPS = (
    (
        along_z([(0, 1), (2, 3), (4, 5), (6, 7)]),
        along_z([(0, 2), (1, 3), (4, 6), (5, 7)]),
        along_z([(0, 3), (1, 2), (4, 7), (5, 6)]),
    ),
    (along_z([(0, 7), (1, 6), (2, 5), (3, 4)]),),
)
BOTH = [
    [(8 * x + z) * 8 + t for x in pair for t in range(8)] for pair in ((0, 1), (2, 3)) for z in range(8)
]


def local(momentum, grad):
    row_enc, col_enc, row_dec, col_dec = (jnp.asarray(t) for t in tables())
    momentum, grad = momentum[0], grad[0]
    moment, bands, keep, send = encode(momentum, grad, row_enc, col_enc)
    new_momentum = residual(moment, bands, row_dec, col_dec)
    own = (
        keep
        + lax.ppermute(send, "dp", HALVES)
        + lax.ppermute(send, "dp", along_x([(1, 2), (3, 0)]))
        + lax.ppermute(keep, "dp", along_x([(0, 2), (1, 3)]))
    )
    for step in STEPS:
        own = sum((lax.ppermute(own, "dp", pairs) for pairs in step), own)
    other = lax.ppermute(own, "dp", HALVES)
    squares = jnp.sum((own * own).reshape(-1, 8, 128), axis=0)
    energy = lax.all_to_all(
        jnp.broadcast_to(squares[None], (16, 8, 128)), ("dp", "tensor"), 0, 0, axis_index_groups=BOTH
    )
    update = decode(spread(own, other, col_dec), energy.reshape(128, 128), row_dec)
    return (new_momentum[None], update)


def solution(mesh):
    return jax.shard_map(
        local,
        mesh=mesh,
        in_specs=(P("dp", None, "tensor"), P("dp", None, "tensor")),
        out_specs=(P("dp", None, "tensor"), P(None, "tensor")),
        check_vma=False,
    )
```

```python
import math

import jax
import jax.numpy as jnp
import ml_dtypes
import numpy as np
from jax import lax
from jax.experimental import pallas as pl
from jax.experimental.pallas import tpu as pltpu
from jax.sharding import PartitionSpec as P

FF = 28672
ROWS = 128
CHUNK = 512
F32 = jnp.float32
BF16 = jnp.bfloat16
HBM = pl.BlockSpec(memory_space=pltpu.HBM)
VMEM = pl.BlockSpec(memory_space=pltpu.VMEM)


def lowband():
    samples = np.arange(32, dtype=np.float64)
    freqs = np.arange(8, dtype=np.float64)
    weights = np.where(freqs == 0.0, math.sqrt(1.0 / 32.0), math.sqrt(2.0 / 32.0))
    return weights[:, None] * np.cos(math.pi * (2.0 * samples[None] + 1.0) * freqs[:, None] / 64.0)


def split(values):
    high = values.astype(ml_dtypes.bfloat16)
    low = (values - high.astype(np.float64)).astype(ml_dtypes.bfloat16)
    return high, low


def tables():
    low = lowband()
    row_high, row_low = split(np.kron(np.eye(ROWS // 32), low))
    col_high, col_low = split(np.kron(np.eye(CHUNK // 32), low.T))
    zero = np.zeros_like(row_high)
    row_enc = np.block([[row_high, row_high], [row_low, zero]])
    col_enc = np.concatenate([col_high, col_low], axis=1)
    row_dec = np.concatenate([row_high.T, row_high.T, row_low.T], axis=1)
    pad = np.zeros((ROWS, 32), ml_dtypes.bfloat16)
    row_dec = np.concatenate([row_dec, pad], axis=1)
    col_dec = np.concatenate([col_high.T, col_high.T, col_low.T], axis=0)
    return row_enc, col_enc, row_dec, col_dec


def dot(a, b):
    return jnp.dot(a, b, preferred_element_type=F32)


def halves(x):
    high = x.astype(BF16)
    return high, (x - high.astype(F32)).astype(BF16)


def ordered(first, second):
    odd = lax.rem(lax.axis_index("dp") // 8, 2) == 1
    return jnp.where(odd, second, first), jnp.where(odd, first, second)


def encode_kernel(
    chunks, m_hbm, g_hbm, row_hbm, col_hbm, moment_ref, bands_ref, keep_ref, send_ref, m, g, row, col, mixed, sems
):
    copies = []
    for i in range(chunks):
        cols = pl.ds(i * CHUNK, CHUNK)
        copies.append(
            (
                pltpu.make_async_copy(m_hbm.at[:, cols], m.at[i], sems.at[0, i]),
                pltpu.make_async_copy(g_hbm.at[:, cols], g.at[i], sems.at[1, i]),
            )
        )
    tables_in = (
        pltpu.make_async_copy(row_hbm, row, sems.at[0, chunks]),
        pltpu.make_async_copy(col_hbm, col, sems.at[1, chunks]),
    )
    tables_in[0].start()
    for pair in copies:
        pair[0].start()
        pair[1].start()
    tables_in[1].start()
    tables_in[0].wait()
    for group in (range(1), range(1, chunks // 2 + 1), range(chunks // 2 + 1, chunks)):
        for i in group:
            copies[i][0].wait()
            copies[i][1].wait()
        for i in group:
            moment = 0.999 * m[i] + g[i].astype(F32)
            moment_ref[i] = moment
            both = dot(row[...], jnp.concatenate(halves(moment), axis=0))
            mixed[pl.ds(i * 32, 32), :] = both[:32] + both[32:]
    tables_in[1].wait()
    high, low = halves(mixed[...])
    first = dot(high, col[...])
    bands = first[:, :128] + first[:, 128:] + dot(low, col[:, :128])
    bands_ref[...] = bands
    half = bands.shape[0] // 2
    keep_ref[...], send_ref[...] = ordered(bands[:half], bands[half:])


def expand(bands, col):
    high, low = halves(bands)
    return dot(jnp.concatenate([high, low, high], axis=1), col)


def stacked(part):
    high, low = halves(part)
    return jnp.concatenate([high, low, high, jnp.zeros_like(high)], axis=0)


def rows_of(part, row):
    return dot(row, stacked(part))


def residual_kernel(chunks, moment_ref, bands_ref, row_ref, col_ref, out_hbm, out, spread, sems):
    spread[...] = expand(bands_ref[...], col_ref[...])
    stores = []
    for i in range(chunks):
        cols = pl.ds(i * CHUNK, CHUNK)
        out[i] = moment_ref[i] - rows_of(spread[pl.ds(i * 32, 32), :], row_ref[...])
        stores.append(pltpu.make_async_copy(out.at[i], out_hbm.at[:, cols], sems.at[i]))
        stores[-1].start()
    for store in stores:
        store.wait()


def spread_kernel(chunks, own_ref, other_ref, col_ref, stack_ref):
    bands = jnp.concatenate(ordered(own_ref[...], other_ref[...]), axis=0)
    mixed = expand(bands, col_ref[...])
    for i in range(chunks):
        stack_ref[i] = stacked(mixed[i * 32 : (i + 1) * 32])


def update_kernel(chunks, stack_ref, energy_ref, row_ref, out_hbm, out, sems):
    energy = jnp.sum(energy_ref[...])
    scale = lax.rsqrt(jnp.full((1, CHUNK), energy * (1.0 / (ROWS * FF)) + 1e-06, F32))
    stores = []
    for i in range(chunks):
        cols = pl.ds(i * CHUNK, CHUNK)
        out[i] = dot(row_ref[...], stack_ref[i]) * scale
        stores.append(pltpu.make_async_copy(out.at[i], out_hbm.at[:, cols], sems.at[i]))
        stores[-1].start()
    for store in stores:
        store.wait()


PARAMS = pltpu.CompilerParams(vmem_limit_bytes=24 * 1024 * 1024)


def in_hbm(x):
    return pltpu.with_memory_space_constraint(x, pltpu.HBM)


def encode(m, g, row, col):
    chunks = m.shape[1] // CHUNK
    return pl.pallas_call(
        lambda *refs: encode_kernel(chunks, *refs),
        out_shape=[jax.ShapeDtypeStruct((chunks, ROWS, CHUNK), F32)]
        + [jax.ShapeDtypeStruct((rows, 128), F32) for rows in (chunks * 32, chunks * 16, chunks * 16)],
        in_specs=[HBM] * 4,
        out_specs=[VMEM] * 4,
        scratch_shapes=[
            pltpu.VMEM((chunks, ROWS, CHUNK), F32),
            pltpu.VMEM((chunks, ROWS, CHUNK), BF16),
            pltpu.VMEM(row.shape, BF16),
            pltpu.VMEM(col.shape, BF16),
            pltpu.VMEM((chunks * 32, CHUNK), F32),
            pltpu.SemaphoreType.DMA((2, chunks + 1)),
        ],
        compiler_params=PARAMS,
        cost_estimate=pl.CostEstimate(flops=4 * 10**7, bytes_accessed=3 * 10**6, transcendentals=0),
        name="encode",
    )(*(in_hbm(a) for a in (m, g, row, col)))


def residual(moment, bands, row, col):
    chunks = moment.shape[0]
    return pl.pallas_call(
        lambda *refs: residual_kernel(chunks, *refs),
        out_shape=jax.ShapeDtypeStruct((ROWS, chunks * CHUNK), F32),
        in_specs=[VMEM] * 4,
        out_specs=HBM,
        scratch_shapes=[
            pltpu.VMEM((chunks, ROWS, CHUNK), F32),
            pltpu.VMEM((chunks * 32, CHUNK), F32),
            pltpu.SemaphoreType.DMA((chunks,)),
        ],
        compiler_params=PARAMS,
        cost_estimate=pl.CostEstimate(flops=4 * 10**7, bytes_accessed=5 * 10**6, transcendentals=0),
        name="residual",
    )(moment, bands, row, col)


def spread(own, other, col):
    chunks = own.shape[0] // 16
    return pl.pallas_call(
        lambda *refs: spread_kernel(chunks, *refs),
        out_shape=jax.ShapeDtypeStruct((chunks, 128, CHUNK), BF16),
        in_specs=[VMEM] * 3,
        out_specs=VMEM,
        compiler_params=PARAMS,
        cost_estimate=pl.CostEstimate(flops=4 * 10**7, bytes_accessed=10**6, transcendentals=0),
        name="spread",
    )(own, other, col)


def decode(stack, energy, row):
    chunks = stack.shape[0]
    return pl.pallas_call(
        lambda *refs: update_kernel(chunks, *refs),
        out_shape=jax.ShapeDtypeStruct((ROWS, chunks * CHUNK), F32),
        in_specs=[VMEM] * 3,
        out_specs=HBM,
        scratch_shapes=[
            pltpu.VMEM((chunks, ROWS, CHUNK), F32),
            pltpu.SemaphoreType.DMA((chunks,)),
        ],
        compiler_params=PARAMS,
        cost_estimate=pl.CostEstimate(flops=4 * 10**7, bytes_accessed=2 * 10**6, transcendentals=0),
        name="decode",
    )(stack, energy, row)


def partners(pairs):
    other = {}
    for a, b in pairs:
        other[a], other[b] = b, a
    return other


def along_z(pairs):
    other = partners(pairs)
    return [(8 * x + z, 8 * x + other[z]) for x in range(4) for z in range(8)]


def along_x(pairs):
    other = partners(pairs)
    return [(8 * x + z, 8 * other[x] + z) for x in range(4) for z in range(8)]


HALVES = along_x([(0, 1), (2, 3)])
STEPS = (
    (
        along_z([(0, 1), (2, 3), (4, 5), (6, 7)]),
        along_z([(0, 2), (1, 3), (4, 6), (5, 7)]),
        along_z([(0, 3), (1, 2), (4, 7), (5, 6)]),
    ),
    (along_z([(0, 7), (1, 6), (2, 4), (3, 5)]),),
)
BOTH = [
    [(8 * x + z) * 8 + t for x in pair for t in range(8)] for pair in ((0, 1), (2, 3)) for z in range(8)
]


def local(momentum, grad):
    row_enc, col_enc, row_dec, col_dec = (jnp.asarray(t) for t in tables())
    momentum, grad = momentum[0], grad[0]
    moment, bands, keep, send = encode(momentum, grad, row_enc, col_enc)
    new_momentum = residual(moment, bands, row_dec, col_dec)
    own = (
        keep
        + lax.ppermute(send, "dp", HALVES)
        + lax.ppermute(send, "dp", along_x([(1, 2), (3, 0)]))
        + lax.ppermute(keep, "dp", along_x([(0, 2), (1, 3)]))
    )
    for step in STEPS:
        own = sum((lax.ppermute(own, "dp", pairs) for pairs in step), own)
    other = lax.ppermute(own, "dp", HALVES)
    squares = jnp.sum((own * own).reshape(-1, 8, 128), axis=0)
    energy = lax.all_to_all(
        jnp.broadcast_to(squares[None], (16, 8, 128)), ("dp", "tensor"), 0, 0, axis_index_groups=BOTH
    )
    update = decode(spread(own, other, col_dec), energy.reshape(128, 128), row_dec)
    return (new_momentum[None], update)


def solution(mesh):
    return jax.shard_map(
        local,
        mesh=mesh,
        in_specs=(P("dp", None, "tensor"), P("dp", None, "tensor")),
        out_specs=(P("dp", None, "tensor"), P(None, "tensor")),
        check_vma=False,
    )
```
